128 devices in a mesh: dp: 4 (over y_lo, core), pipe: 4 (over z), seq: 8 (over y_hi, x).
Axes of the slice: x: 4, y: 4 (y_hi: 2, y_lo: 2; y = y_hi * 2 + y_lo), z: 4, core: 2. Of those that a mesh axis runs over, the one named last changes fastest.
Arguments:
- layer_input: bfloat16 [4, 4, 2048, 4096], P('dp', 'pipe', 'seq'), may hold values from -0.09375 to 0.09375
- queries: bfloat16 [4, 4, 2048, 4096], P('dp', 'pipe', 'seq'), may hold values from -6 to 6
- keys: bfloat16 [4, 4, 2048, 512], P('dp', 'pipe', 'seq'), may hold values from -6 to 6
- values: bfloat16 [4, 4, 2048, 512], P('dp', 'pipe', 'seq'), may hold values from -6 to 6
- attn_out: bfloat16 [4, 4, 2048, 4096], P('dp', 'pipe', 'seq'), may hold values from -6 to 6
- out_grad: bfloat16 [4, 4, 2048, 4096], P('dp', 'pipe', 'seq'), may hold values from -6 to 6
- log_norm: bfloat16 [4, 4, 2048, 32], P('dp', 'pipe', 'seq'), may hold values from 2 to 6
- segment_ids: int32 [4, 4, 2048], P('dp', 'pipe'), may hold values from 0 to 7, never falling along the last dimension, each value on 1 to 1024 neighbouring positions
- key_weight: bfloat16 [4, 4096, 512], P('pipe'), may hold values from -0.25 to 0.25
- value_weight: bfloat16 [4, 4096, 512], P('pipe'), may hold values from -0.25 to 0.25
Outputs:
- query_grad: bfloat16 [4, 4, 2048, 4096], P('dp', 'pipe', 'seq')
- upstream_grad: bfloat16 [4, 4, 2048, 4096], P('dp', 'pipe', 'seq')
- key_weight_grad: float32 [4, 4096, 512], P('pipe', ('dp', 'seq'))
- value_weight_grad: float32 [4, 4096, 512], P('pipe', ('dp', 'seq'))
The draws below stay inside these ranges and needn't reach their ends.
Inputs may be any that keep to these rules, and one draw needn't show every extreme that they name: `segment_ids`: along each sequence the document ids never fall; each document holds 1 to 1024 tokens, and one holds exactly 1024.
All inputs are finite; a program needn't handle non-finite values.
Results may differ from the reference program's by a relative error of at most 0.0063.
Values may be sent and summed in bfloat16 or wider, within the bound.
A program may use at most 128 MiB of HBM per device.

```python
import math
import jax
import jax.numpy as jnp
import numpy as np
from jax import lax

D = 4096
HQ = 32
KVH = 4
HD = 128
DOCS = 8
TOK_DEV = 256
SEQ_LEN = 2048
QC = 4096
KVC = 512
N_DP = 4
N_PIPE = 4
N_SEQ = 8


def raised(result, stream_key, source, target, parts, factor):
    def block_of(axis_at):
        return (jnp.arange(result.shape[axis_at]) // (result.shape[axis_at] // parts)).reshape((-1,) + (1,) * (result.ndim - 1 - axis_at))

    one_side = jax.random.permutation(stream_key, parts)[block_of(target)]
    other_side = (block_of(target) + parts // 2) % parts
    return jnp.where((block_of(source) == one_side) | (block_of(source) == other_side), factor * result, result)


def block_scale(key, shape, shards, least, largest):
    level = 1.0
    for axis_at, blocks in shards:
        draws = jax.random.uniform(jax.random.fold_in(jax.random.fold_in(key, 6), axis_at), (blocks,), jnp.float32, least / len(shards), largest / len(shards))
        level = level * jnp.repeat(jnp.exp(draws), shape[axis_at] // blocks).reshape((-1,) + (1,) * (len(shape) - 1 - axis_at))
    return level


def profile(count, total, most, lean):
    portions = [(1 << 20) // math.isqrt(standing ** lean) + 1 for standing in range(2, count + 1)]
    spare, given = total - most - (count - 1), [1] * (count - 1)
    while spare > 0:
        movable = [i for i in range(count - 1) if given[i] < most]
        mass, left = sum([portions[i] for i in movable]), spare
        for i in movable:
            extra = min(most - given[i], max(1, left * portions[i] // mass), spare)
            given[i] = given[i] + extra
            spare = spare - extra
    return np.array([most] + given)


def ragged_sizes(own_key, count, total, bound, slope):
    if count == 2:
        one = jax.random.randint(own_key, (), max(1, total - bound), min(bound, total - 1) + 1)
        return jnp.stack([one, total - one])
    lengths = jnp.asarray(profile(count, total, bound, slope), jnp.int32)
    couples = (count - 1) // 2
    donor, receiver = lengths[1:1 + 2 * couples:2], lengths[2:2 + 2 * couples:2]
    slack = jnp.minimum(donor - 1, bound - receiver)
    shifted = jax.random.randint(jax.random.fold_in(own_key, 1), (couples,), 0, 1 << 20) % (slack + 1)
    lengths = lengths.at[1:1 + 2 * couples:2].set(donor - shifted).at[2:2 + 2 * couples:2].set(receiver + shifted)
    return lengths[jax.random.permutation(jax.random.fold_in(own_key, 2), count)]


def normal_values(stream_key, extent, deviation, reach, cuts=(), kind=jnp.bfloat16):
    values = jax.random.normal(stream_key, extent, jnp.float32) * deviation
    if len(cuts) > 0:
        values = block_scale(stream_key, extent, cuts, -0.22, 0.18) * values
    return jnp.clip(values, min=-reach, max=reach).astype(kind)


def bell_draw_with(key, shape, scale, most, pieces, heavy, kind=jnp.bfloat16):
    entries = scale * jax.random.normal(key, shape, jnp.float32)
    if pieces:
        entries = entries * block_scale(key, shape, pieces, -0.22, 0.18)
    return jnp.clip(raised(entries, jax.random.fold_in(key, 3), *heavy), -most, most).astype(kind)


def setup_inputs(seed: int = 0) -> dict:
    arg_keys = jax.random.split(jax.random.key(seed), 11)
    return {
        "layer_input": bell_draw_with(arg_keys[0], (N_DP, N_PIPE, SEQ_LEN, D), (TOK_DEV * N_DP * N_SEQ) ** -0.5, 0.09375, ((0, 4), (1, 4), (2, 8)), (2, 3, 8, 2.0)),
        "queries": normal_values(arg_keys[1], (N_DP, N_PIPE, SEQ_LEN, QC), 1.0, 6.0, ((0, 4), (1, 4), (2, 8))),
        "keys": normal_values(arg_keys[2], (N_DP, N_PIPE, SEQ_LEN, KVC), 1.0, 6.0, ((0, 4), (1, 4), (2, 8))),
        "values": normal_values(arg_keys[3], (N_DP, N_PIPE, SEQ_LEN, KVC), 1.0, 6.0, ((0, 4), (1, 4), (2, 8))),
        "attn_out": normal_values(arg_keys[4], (N_DP, N_PIPE, SEQ_LEN, QC), 1.0, 6.0, ((0, 4), (1, 4), (2, 8))),
        "out_grad": normal_values(arg_keys[5], (N_DP, N_PIPE, SEQ_LEN, QC), 1.0, 6.0, ((0, 4), (1, 4), (2, 8))),
        "log_norm": jnp.clip(2.0 + 4.0 * jax.random.uniform(arg_keys[6], (N_DP, N_PIPE, SEQ_LEN, HQ), jnp.float32) ** block_scale(arg_keys[6], (N_DP, N_PIPE, SEQ_LEN, HQ), ((0, 4), (1, 4), (2, 8)), -0.2, 0.2), 2.0, 6.0).astype(jnp.bfloat16),
        "segment_ids": jax.vmap(lambda own: jnp.searchsorted(jnp.cumsum(ragged_sizes(own, DOCS, SEQ_LEN, SEQ_LEN // 2, 1)), jnp.arange(SEQ_LEN), side="right"))(jax.random.split(arg_keys[7], N_DP * N_PIPE)).reshape((N_DP, N_PIPE, SEQ_LEN)).astype(jnp.int32),
        "key_weight": normal_values(arg_keys[8], (N_PIPE, D, KVC), KVC ** -0.5, 0.25, ((0, 4),)),
        "value_weight": normal_values(arg_keys[9], (N_PIPE, D, KVC), KVC ** -0.5, 0.25, ((0, 4),)),
    }


def attend(query_block, grad_block, norm_block, delta_block, row_seg, row_pos, head_keys, head_values, col_seg, col_pos):
    score_scale = 1.0 / math.sqrt(HD)
    scores = lax.dot_general(query_block, head_keys, (((1,), (1,)), ((), ())), preferred_element_type=jnp.float32) * score_scale
    allowed = (row_seg[:, None] == col_seg[None, :]) & (col_pos[None, :] <= row_pos[:, None])
    probability = jnp.exp(jnp.where(allowed, scores - norm_block.astype(jnp.float32)[:, None], -1e+30))
    grad_v = lax.dot_general(probability.astype(jnp.bfloat16), grad_block, (((0,), (0,)), ((), ())), preferred_element_type=jnp.float32)
    grad_prob = lax.dot_general(grad_block, head_values, (((1,), (1,)), ((), ())), preferred_element_type=jnp.float32)
    grad_score = (probability * (grad_prob - delta_block.astype(jnp.float32)[:, None])).astype(jnp.bfloat16)
    grad_q = jnp.dot(grad_score, head_keys, preferred_element_type=jnp.float32) * score_scale
    grad_k = lax.dot_general(grad_score, query_block, (((0,), (0,)), ((), ())), preferred_element_type=jnp.float32) * score_scale
    return (grad_q, grad_k, grad_v)

def one_instance(item):
    inputs, query_rows, key_rows, value_rows, out_rows, grad_rows, norm_rows, segments, weight_k, weight_v = item
    positions = jnp.arange(SEQ_LEN, dtype=jnp.int32)
    group_size = HQ // KVH
    product = grad_rows.astype(jnp.float32) * out_rows.astype(jnp.float32)
    delta = lax.optimization_barrier(jnp.sum(product.reshape(SEQ_LEN, HQ, HD), axis=-1)).astype(jnp.bfloat16)

    def one_head(head_index):
        kv_index = head_index // group_size
        head_keys = lax.dynamic_slice_in_dim(key_rows, kv_index * HD, HD, 1)
        head_values = lax.dynamic_slice_in_dim(value_rows, kv_index * HD, HD, 1)
        col_q = lax.dynamic_slice_in_dim(query_rows, head_index * HD, HD, 1)
        col_grad = lax.dynamic_slice_in_dim(grad_rows, head_index * HD, HD, 1)
        col_norm = lax.dynamic_index_in_dim(norm_rows, head_index, 1, keepdims=False)
        col_delta = lax.dynamic_index_in_dim(delta, head_index, 1, keepdims=False)
        return attend(col_q, col_grad, col_norm, col_delta, segments, positions, head_keys, head_values, segments, positions)
    stacked_q, stacked_k, stacked_v = lax.map(one_head, jnp.arange(HQ, dtype=jnp.int32))
    query_grad = stacked_q.transpose(1, 0, 2).reshape(SEQ_LEN, HQ * HD).astype(jnp.bfloat16)
    key_grad = stacked_k.reshape(KVH, group_size, SEQ_LEN, HD).sum(1).transpose(1, 0, 2).reshape(SEQ_LEN, KVH * HD).astype(jnp.bfloat16)
    value_grad = stacked_v.reshape(KVH, group_size, SEQ_LEN, HD).sum(1).transpose(1, 0, 2).reshape(SEQ_LEN, KVH * HD).astype(jnp.bfloat16)
    local_wk = lax.dot_general(inputs, key_grad, (((0,), (0,)), ((), ())), preferred_element_type=jnp.float32)
    local_wv = lax.dot_general(inputs, value_grad, (((0,), (0,)), ((), ())), preferred_element_type=jnp.float32)
    input_grad = lax.dot_general(key_grad, weight_k, (((1,), (1,)), ((), ())), preferred_element_type=jnp.float32)
    input_grad = input_grad + lax.dot_general(value_grad, weight_v, (((1,), (1,)), ((), ())), preferred_element_type=jnp.float32)
    return (query_grad, input_grad.astype(jnp.bfloat16), local_wk, local_wv)

def flatten_pair(array):
    return array.reshape((N_DP * N_PIPE,) + array.shape[2:])

def reference(layer_input, queries, keys, values, attn_out, out_grad, log_norm, segment_ids, key_weight, value_weight):
    wide_k = jnp.broadcast_to(key_weight[None], (N_DP,) + key_weight.shape)
    wide_v = jnp.broadcast_to(value_weight[None], (N_DP,) + value_weight.shape)
    arrays = (layer_input, queries, keys, values, attn_out, out_grad, log_norm, segment_ids, wide_k, wide_v)
    items = tuple((flatten_pair(array) for array in arrays))
    query_grad, input_grad, local_wk, local_wv = lax.map(one_instance, items)
    query_grad = query_grad.reshape(N_DP, N_PIPE, SEQ_LEN, HQ * HD)
    input_grad = input_grad.reshape(N_DP, N_PIPE, SEQ_LEN, D)
    upstream_grad = jnp.concatenate([input_grad[:, 1:], jnp.zeros_like(input_grad[:, :1])], axis=1)
    key_weight_grad = local_wk.reshape(N_DP, N_PIPE, D, KVH * HD).sum(0)
    value_weight_grad = local_wv.reshape(N_DP, N_PIPE, D, KVH * HD).sum(0)
    return (query_grad, upstream_grad, key_weight_grad, value_weight_grad)
```

```python
import functools
import math

import jax
import jax.numpy as jnp
from jax import lax
from jax.experimental import pallas as pl
from jax.experimental.pallas import tpu as pltpu
from jax.sharding import PartitionSpec as P

HQ = 32
KVH = 4
GROUP = HQ // KVH
HD = 128
TOK = 256
HALF = 128
D = 4096
NEAR = 4
SCALE = 1.0 / math.sqrt(HD)
LOG2E = math.log2(math.e)
MASKED = -1e30
MESH = pl.DeviceIdType.MESH
BF = jnp.bfloat16
F32 = jnp.float32


def dot(a, b, ca, cb):
    return lax.dot_general(a, b, (((ca,), (cb,)), ((), ())), preferred_element_type=F32)


def kernel(
    x_hbm, q_hbm, k_hbm, v_hbm, o_hbm, g_hbm, norm_hbm, seg_hbm, wk_hbm, wv_hbm,
    dq_hbm, up_hbm, gk_hbm, gv_hbm,
    q, g, o, norm_in, seg, wk, wv, kv, norm, delta, bias, dqt, dq,
    part_out, part_in, own, grads, pair, xb, up, zeros,
    xs_out, xs_in, ys_out, ys_in, x_own, y_own, x2_out, x2_in, y2_out, y2_in, x_fin, y_fin, gk, gv,
    in_sem, kv_local, xb_local, xb_send, xb_recv, kv_send, kv_recv, part_send, part_recv,
    pair_send, pair_recv, z_send, z_recv, xs_send, xs_recv, ys_send, ys_recv,
    x2_send, x2_recv, y2_send, y2_recv, out_sem,
):
    dp = lax.axis_index("dp")
    p = lax.axis_index("pipe")
    s = lax.axis_index("seq")
    core = lax.rem(dp, 2)
    y_lo = dp // 2
    y_hi = s // 4
    x_at = lax.rem(s, 4)
    y_at = y_hi * 2 + y_lo

    def chip(x, y):
        return (lax.rem(y, 2) * 2 + core, p, (y // 2) * 4 + x)

    def along_x(step):
        return chip(lax.rem(x_at + step, 4), y_at)

    def along_y(step):
        return chip(x_at, lax.rem(y_at + step, 4))

    partner = (y_lo * 2 + 1 - core, p, s)

    def kv_copies():
        for half in range(2):
            for head in range(KVH):
                for which, ref in ((0, k_hbm), (1, v_hbm)):
                    yield pltpu.make_async_copy(
                        ref.at[pl.ds(half * HALF, HALF), pl.ds(head * HD, HD)],
                        kv.at[half, head, which, 0],
                        kv_local.at[half, head, which],
                    )

    copies = list(kv_copies())
    for copy in copies:
        copy.start()
    loads = [
        pltpu.make_async_copy(source, target, in_sem.at[i])
        for i, (source, target) in enumerate(
            ((norm_hbm, norm_in), (seg_hbm, seg), (g_hbm, g), (o_hbm, o), (q_hbm, q), (wk_hbm, wk), (wv_hbm, wv))
        )
    ]
    for copy in loads:
        copy.start()

    def x_columns(block, owner_core):
        y = lax.rem(y_at + block // 4, 4)
        x = lax.rem(x_at + block % 4, 4)
        row = (lax.rem(y, 2) * 2 + owner_core) * 1024 + (y // 2) * 512 + x * 128
        return pl.ds(pl.multiple_of(row, 128), 128)

    def xb_copy(block):
        return pltpu.make_async_copy(
            x_hbm.at[:, x_columns(block, core)], xb.at[0, :, pl.ds(block * 128, 128)], xb_local.at[block]
        )

    def xb_remote(block):
        return pltpu.make_async_remote_copy(
            src_ref=x_hbm.at[:, x_columns(block, 1 - core)],
            dst_ref=xb.at[1, :, pl.ds(block * 128, 128)],
            send_sem=xb_send.at[block],
            recv_sem=xb_recv.at[block],
            device_id=partner,
            device_id_type=MESH,
        )

    def kv_remote(dist, half, head):
        return pltpu.make_async_remote_copy(
            src_ref=kv.at[half, head, :, 0],
            dst_ref=kv.at[half, head, :, dist],
            send_sem=kv_send.at[dist - 1, half, head],
            recv_sem=kv_recv.at[dist - 1, half, head],
            device_id=(dp, p, lax.rem(s + dist, 8)),
            device_id_type=MESH,
        )

    def part_remote(dist, half, head):
        return pltpu.make_async_remote_copy(
            src_ref=part_out.at[half, head, dist - 1],
            dst_ref=part_in.at[half, head, dist - 1],
            send_sem=part_send.at[dist - 1, half, head],
            recv_sem=part_recv.at[dist - 1, half, head],
            device_id=(dp, p, lax.rem(s + 8 - dist, 8)),
            device_id_type=MESH,
        )

    def pair_remote(half, head):
        return pltpu.make_async_remote_copy(
            src_ref=pair.at[head, 0, half],
            dst_ref=pair.at[head, 1, half],
            send_sem=pair_send.at[half, head],
            recv_sem=pair_recv.at[half, head],
            device_id=partner,
            device_id_type=MESH,
        )

    def z_remote(half, chunk):
        return pltpu.make_async_remote_copy(
            src_ref=up.at[pl.ds(half * HALF, HALF), pl.ds(chunk * 1024, 1024)],
            dst_ref=up_hbm.at[pl.ds(half * HALF, HALF), pl.ds(chunk * 1024, 1024)],
            send_sem=z_send.at[half, chunk],
            recv_sem=z_recv.at[half, chunk],
            device_id=(dp, lax.rem(p + 3, 4), s),
            device_id_type=MESH,
        )

    def spread(source, target, send, recv, reach, head, step):
        return pltpu.make_async_remote_copy(
            src_ref=source.at[head, step - 1],
            dst_ref=target.at[head, step - 1],
            send_sem=send.at[head, step - 1],
            recv_sem=recv.at[head, step - 1],
            device_id=reach(step),
            device_id_type=MESH,
        )

    x_first = functools.partial(spread, xs_out, xs_in, xs_send, xs_recv, along_x)
    y_first = functools.partial(spread, ys_out, ys_in, ys_send, ys_recv, along_y)
    x_second = functools.partial(spread, x2_out, x2_in, x2_send, x2_recv, along_y)
    y_second = functools.partial(spread, y2_out, y2_in, y2_send, y2_recv, along_x)

    barrier = pltpu.get_barrier_semaphore()
    peers = [(dp, p, lax.rem(s + i, 8)) for i in range(1, 8)]
    peers += [along_y(i) for i in range(1, 4)]
    peers += [partner, (dp, lax.rem(p + 1, 4), s), (dp, lax.rem(p + 3, 4), s)]
    for peer in peers:
        pl.semaphore_signal(barrier, inc=1, device_id=peer, device_id_type=MESH)
    for copy in copies:
        copy.wait()
    pl.semaphore_wait(barrier, len(peers))

    for half in range(2):
        for head in range(KVH):
            for dist in range(1, NEAR + 1):

                @pl.when(s + dist <= 7)
                def _(dist=dist, half=half, head=head):
                    kv_remote(dist, half, head).start()

                @pl.when(s < dist)
                def _(dist=dist, half=half, head=head):
                    kv[half, head, :, dist] = jnp.zeros((2, HALF, HD), BF)

    for block in range(16):
        xb_copy(block).start()
        xb_remote(block).start()

    loads[0].wait()
    loads[1].wait()
    eye = (
        lax.broadcasted_iota(jnp.int32, (HQ, HQ), 0) == lax.broadcasted_iota(jnp.int32, (HQ, HQ), 1)
    ).astype(F32).astype(BF)
    norm_rows = dot(eye, norm_in[...], 1, 1) * LOG2E
    for head in range(HQ):
        norm[head] = jnp.broadcast_to(norm_rows[head : head + 1], (8, TOK))

    row_seg = seg[:, pl.ds(pl.multiple_of(s * TOK, TOK), TOK)].astype(F32)
    row_seg = jnp.broadcast_to(row_seg, (HALF, TOK))
    row_number = lax.broadcasted_iota(jnp.int32, (HALF, TOK), 1)
    key_number = lax.broadcasted_iota(jnp.int32, (HALF, TOK), 0)

    def document_bias(dist, half):
        block = lax.rem(s + 8 - dist, 8)
        at = pl.multiple_of(block * TOK + half * HALF, HALF)
        key_seg = jnp.broadcast_to(seg[:, pl.ds(at, HALF)].astype(F32), (HALF, HALF)).T
        same = jnp.concatenate([key_seg, key_seg], axis=1) == row_seg
        reach = jnp.where(s >= dist, 0.0, MASKED).astype(F32)
        return jnp.where(same, 0.0, MASKED) + reach

    for half in range(2):
        causal = key_number + half * HALF <= row_number
        bias[half, 0:HALF] = jnp.where(causal, document_bias(0, half), document_bias(NEAR, half))
        for dist in range(1, NEAR):
            bias[half, dist * HALF : (dist + 1) * HALF] = document_bias(dist, half)

    loads[2].wait()
    loads[3].wait()
    ones = jnp.ones((8, HD), BF)

    def delta_head(head, carry):
        at = pl.ds(pl.multiple_of(head * HD, HD), HD)
        product = g[:, at].astype(F32) * o[:, at].astype(F32)
        high = product.astype(BF)
        rest = product - high.astype(F32)
        middle = rest.astype(BF)
        low = (rest - middle.astype(F32)).astype(BF)
        total = dot(ones, high, 1, 1) + dot(ones, middle, 1, 1) + dot(ones, low, 1, 1)
        delta[head] = total.astype(BF).astype(F32)
        return carry

    lax.fori_loop(0, HQ, delta_head, 0, unroll=4)
    loads[4].wait()

    @pl.when(p == 3)
    def _():
        zeros[...] = jnp.zeros((TOK, D), BF)
        fill = pltpu.make_async_copy(zeros, up_hbm, out_sem.at[3])
        fill.start()
        fill.wait()

    def finalize(half, head):
        for dist in range(1, NEAR + 1):

            @pl.when(s + dist <= 7)
            def _(dist=dist):
                part_remote(dist, half, head).wait_recv()
                own[half, head] += part_in[half, head, dist - 1].astype(F32)

        total = own[half, head].astype(BF)
        at = pl.multiple_of(head * HD, HD)
        grads[half, :, pl.ds(at, HD)] = total[0]
        grads[half, :, pl.ds(pl.multiple_of(at + KVH * HD, HD), HD)] = total[1]
        pair[head, 0, half, :, 0:HD] = total[0]
        pair[head, 0, half, :, HD : 2 * HD] = total[1]
        pair_remote(half, head).start()

    def input_grad(half):
        if half == 0:
            loads[5].wait()
            loads[6].wait()
        rows = pl.ds(half * HALF, HALF)

        def chunk_step(chunk, carry):
            for part in range(2):
                at = pl.ds(pl.multiple_of(chunk * 1024 + part * 512, 512), 512)
                total = dot(grads[half, :, 0 : KVH * HD], wk[at, :], 1, 1)
                total = total + dot(grads[half, :, KVH * HD : 2 * KVH * HD], wv[at, :], 1, 1)
                up[rows, at] = total.astype(BF)

            @pl.when(p > 0)
            def _():
                z_remote(half, chunk).start()

            return carry

        lax.fori_loop(0, 4, chunk_step, 0)

    def weight_terms(head):
        pair_remote(0, head).wait_recv()
        pair_remote(1, head).wait_recv()
        both = pair[head].reshape(2 * TOK, 2 * HD)

        def row_of_targets(ry):
            at = pl.ds(ry * 512, 512)
            terms = dot(both, xb[:, :, at].reshape(2 * TOK, 512), 0, 0)
            x_own[head, ry] = terms[0:HD, 0:HD]
            for rx in range(1, 4):
                xs_out[head, rx - 1, ry] = terms[0:HD, rx * HD : (rx + 1) * HD].astype(BF)
            for rx in range(4):
                if ry == 0:
                    y_own[head, rx] = terms[HD : 2 * HD, rx * HD : (rx + 1) * HD]
                else:
                    ys_out[head, ry - 1, rx] = terms[HD : 2 * HD, rx * HD : (rx + 1) * HD].astype(BF)

        for ry in range(4):
            row_of_targets(ry)
        for step in range(1, 4):
            x_first(head, step).start()
            y_first(head, step).start()

    def weight_sums(head):
        for step in range(1, 4):
            x_first(head, step).wait_recv()
            y_first(head, step).wait_recv()
        for r in range(4):
            total = x_own[head, r]
            other = y_own[head, r]
            for step in range(3):
                total = total + xs_in[head, step, r].astype(F32)
                other = other + ys_in[head, step, r].astype(F32)
            if r == 0:
                x_fin[head] = total
                y_fin[head] = other
            else:
                x2_out[head, r - 1] = total.astype(BF)
                y2_out[head, r - 1] = other.astype(BF)
        for step in range(1, 4):
            x_second(head, step).start()
            y_second(head, step).start()

    def weight_final(head):
        for step in range(1, 4):
            x_second(head, step).wait_recv()
            y_second(head, step).wait_recv()
        total = x_fin[head]
        other = y_fin[head]
        for step in range(3):
            total = total + x2_in[head, step].astype(F32)
            other = other + y2_in[head, step].astype(F32)
        at = pl.ds(pl.multiple_of(head * HD, HD), HD)
        gk[:, at] = total.T
        gv[:, at] = other.T

    def attend(half, head, middle):
        for dist in range(1, NEAR + 1):

            @pl.when(s >= dist)
            def _(dist=dist):
                kv_remote(dist, half, head).wait_recv()

        keys = kv[half, head, 0].reshape((NEAR + 1) * HALF, HD)
        values = kv[half, head, 1].reshape((NEAR + 1) * HALF, HD)
        keys_t = keys.T
        causal = key_number + half * HALF <= row_number
        total_k = jnp.zeros(((NEAR + 1) * HALF, HD), F32)
        total_v = jnp.zeros(((NEAR + 1) * HALF, HD), F32)
        last = NEAR * HALF
        for i in range(GROUP):
            at = pl.ds(pl.multiple_of(head * (GROUP * HD) + i * HD, HD), HD)
            q_head = q[:, at]
            g_head = g[:, at]
            number = head * GROUP + i
            scores = dot(keys, q_head, 1, 1)
            scores = jnp.concatenate(
                [jnp.where(causal, scores[0:HALF], scores[last:]), scores[HALF:last]], axis=0
            )
            prob = jnp.exp2(scores * (SCALE * LOG2E) - norm[number][0:1] + bias[half])
            grad_prob = dot(values, g_head, 1, 1)
            grad_prob = jnp.concatenate(
                [jnp.where(causal, grad_prob[0:HALF], grad_prob[last:]), grad_prob[HALF:last]], axis=0
            )
            grad_score = prob * (grad_prob - delta[number][0:1])

            def apart(array):
                first = array[0:HALF]
                return jnp.concatenate(
                    [
                        jnp.where(causal, first, 0.0).astype(BF),
                        array[HALF:last].astype(BF),
                        jnp.where(causal, 0.0, first).astype(BF),
                    ],
                    axis=0,
                )

            prob = apart(prob)
            grad_score = apart(grad_score)
            total_v = total_v + dot(prob, g_head, 1, 0)
            total_k = total_k + dot(grad_score, q_head, 1, 0)
            grad_q = dot(keys_t, grad_score, 1, 0)
            if half == 0:
                dqt[number] = grad_q
            else:
                dq[:, at] = ((dqt[number] + grad_q) * SCALE).T.astype(BF)
            if i == GROUP // 2 - 1:
                middle()
        total_k = total_k * SCALE
        own[half, head, 0] = total_k[0:HALF]
        own[half, head, 1] = total_v[0:HALF]
        for dist in range(1, NEAR + 1):
            part_out[half, head, dist - 1, 0] = total_k[dist * HALF : (dist + 1) * HALF].astype(BF)
            part_out[half, head, dist - 1, 1] = total_v[dist * HALF : (dist + 1) * HALF].astype(BF)

            @pl.when(s >= dist)
            def _(dist=dist):
                part_remote(dist, half, head).start()

    def first_half(head, carry):
        def middle():
            @pl.when(head > 0)
            def _():
                finalize(0, head - 1)

        attend(0, head, middle)
        return carry

    lax.fori_loop(0, KVH, first_half, 0)

    for block in range(16):
        xb_copy(block).wait()
        xb_remote(block).wait_recv()

    def second_half(head, carry):
        def middle():
            @pl.when(head == 0)
            def _():
                finalize(0, KVH - 1)
                input_grad(0)

            @pl.when(head > 0)
            def _():
                finalize(1, head - 1)

        attend(1, head, middle)

        @pl.when(head > 0)
        def _():
            weight_terms(head - 1)

        @pl.when(head > 1)
        def _():
            weight_sums(head - 2)

        return carry

    lax.fori_loop(0, KVH, second_half, 0)
    store_dq = pltpu.make_async_copy(dq, dq_hbm, out_sem.at[0])
    store_dq.start()
    finalize(1, KVH - 1)
    input_grad(1)
    weight_terms(KVH - 1)
    weight_sums(KVH - 2)
    weight_sums(KVH - 1)

    def finish(head, carry):
        weight_final(head)
        return carry

    lax.fori_loop(0, KVH, finish, 0)
    store_gk = pltpu.make_async_copy(gk, gk_hbm, out_sem.at[1])
    store_gv = pltpu.make_async_copy(gv, gv_hbm, out_sem.at[2])
    store_gk.start()
    store_gv.start()

    for half in range(2):

        def sent(head, carry, half=half):
            for dist in range(1, NEAR + 1):

                @pl.when(s + dist <= 7)
                def _(dist=dist):
                    kv_remote(dist, half, head).wait_send()

                @pl.when(s >= dist)
                def _(dist=dist):
                    part_remote(dist, half, head).wait_send()

            pair_remote(half, head).wait_send()

            @pl.when(p > 0)
            def _():
                z_remote(half, head).wait_send()

            @pl.when(p < 3)
            def _():
                z_remote(half, head).wait_recv()

            return carry

        lax.fori_loop(0, 4, sent, 0)

    def sums_sent(head, carry):
        for step in range(1, 4):
            x_first(head, step).wait_send()
            y_first(head, step).wait_send()
            x_second(head, step).wait_send()
            y_second(head, step).wait_send()
        return carry

    lax.fori_loop(0, KVH, sums_sent, 0)
    for block in range(16):
        xb_remote(block).wait_send()
    store_dq.wait()
    store_gk.wait()
    store_gv.wait()


def shards(
    layer_input, queries, keys, values, attn_out, out_grad, log_norm, segment_ids, key_weight, value_weight
):
    any_space = pl.BlockSpec(memory_space=pl.ANY)
    vmem = pltpu.VMEM
    dma = pltpu.SemaphoreType.DMA
    pieces = (2, KVH, NEAR, 2, HALF, HD)
    outs = pl.pallas_call(
        kernel,
        out_shape=(
            jax.ShapeDtypeStruct((TOK, D), BF),
            jax.ShapeDtypeStruct((TOK, D), BF),
            jax.ShapeDtypeStruct((128, KVH * HD), F32),
            jax.ShapeDtypeStruct((128, KVH * HD), F32),
        ),
        in_specs=[any_space] * 10,
        out_specs=(any_space,) * 4,
        scratch_shapes=[
            vmem((TOK, D), BF),
            vmem((TOK, D), BF),
            vmem((TOK, D), BF),
            vmem((TOK, HQ), BF),
            vmem((1, 8 * TOK), jnp.int32),
            vmem((D, KVH * HD), BF),
            vmem((D, KVH * HD), BF),
            vmem((2, KVH, 2, NEAR + 1, HALF, HD), BF),
            vmem((HQ, 8, TOK), F32),
            vmem((HQ, 8, TOK), F32),
            vmem((2, NEAR * HALF, TOK), F32),
            vmem((HQ, HD, TOK), F32),
            vmem((TOK, D), BF),
            vmem(pieces, BF),
            vmem(pieces, BF),
            vmem((2, KVH, 2, HALF, HD), F32),
            vmem((2, HALF, 2 * KVH * HD), BF),
            vmem((KVH, 2, 2, HALF, 2 * HD), BF),
            vmem((2, TOK, 2048), BF),
            vmem((TOK, D), BF),
            vmem((TOK, D), BF),
            vmem((KVH, 3, 4, HD, HD), BF),
            vmem((KVH, 3, 4, HD, HD), BF),
            vmem((KVH, 3, 4, HD, HD), BF),
            vmem((KVH, 3, 4, HD, HD), BF),
            vmem((KVH, 4, HD, HD), F32),
            vmem((KVH, 4, HD, HD), F32),
            vmem((KVH, 3, HD, HD), BF),
            vmem((KVH, 3, HD, HD), BF),
            vmem((KVH, 3, HD, HD), BF),
            vmem((KVH, 3, HD, HD), BF),
            vmem((KVH, HD, HD), F32),
            vmem((KVH, HD, HD), F32),
            vmem((128, KVH * HD), F32),
            vmem((128, KVH * HD), F32),
            dma((7,)),
            dma((2, KVH, 2)),
            dma((16,)),
            dma((16,)),
            dma((16,)),
            dma((NEAR, 2, KVH)),
            dma((NEAR, 2, KVH)),
            dma((NEAR, 2, KVH)),
            dma((NEAR, 2, KVH)),
            dma((2, KVH)),
            dma((2, KVH)),
            dma((2, 4)),
            dma((2, 4)),
        ]
        + [dma((KVH, 3))] * 8
        + [dma((4,))],
        compiler_params=pltpu.CompilerParams(
            collective_id=0, has_side_effects=True, vmem_limit_bytes=60 * 1024 * 1024
        ),
        cost_estimate=pl.CostEstimate(flops=20_000_000_000, bytes_accessed=24_000_000, transcendentals=8_000_000),
        name="attention_backward",
    )(
        layer_input[0, 0], queries[0, 0], keys[0, 0], values[0, 0], attn_out[0, 0], out_grad[0, 0],
        log_norm[0, 0], segment_ids[0], key_weight[0], value_weight[0],
    )
    query_grad, upstream, grad_wk, grad_wv = outs
    return (query_grad[None, None], upstream[None, None], grad_wk[None], grad_wv[None])


def solution(mesh):
    rows = P("dp", "pipe", "seq", None)
    weight = P("pipe", None, None)
    return jax.shard_map(
        shards,
        mesh=mesh,
        in_specs=(rows,) * 7 + (P("dp", "pipe", None), weight, weight),
        out_specs=(rows, rows, P("pipe", ("dp", "seq"), None), P("pipe", ("dp", "seq"), None)),
        check_vma=False,
    )
```

```python
import functools
import math

import jax
import jax.numpy as jnp
from jax import lax
from jax.experimental import pallas as pl
from jax.experimental.pallas import tpu as pltpu
from jax.sharding import PartitionSpec as P

HQ = 32
KVH = 4
GROUP = HQ // KVH
HD = 128
TOK = 256
HALF = 128
D = 4096
NEAR = 4
SCALE = 1.0 / math.sqrt(HD)
LOG2E = math.log2(math.e)
MASKED = -1e30
MESH = pl.DeviceIdType.MESH
BF = jnp.bfloat16
F32 = jnp.float32


def dot(a, b, ca, cb):
    return lax.dot_general(a, b, (((ca,), (cb,)), ((), ())), preferred_element_type=F32)


def kernel(
    x_hbm, q_hbm, k_hbm, v_hbm, o_hbm, g_hbm, norm_hbm, seg_hbm, wk_hbm, wv_hbm,
    dq_hbm, up_hbm, gk_hbm, gv_hbm,
    q, g, o, norm_in, seg, wk, wv, kv, norm, delta, bias, dqt, dq,
    part_out, part_in, relay, own, grads, pair, xb, up, z_pass, zeros,
    xs_out, xs_in, ys_out, ys_in, x_own, y_own, x2_out, x2_in, y2_out, y2_in, x_fin, y_fin, gk, gv,
    in_sem, kv_local, xb_local, xb_send, xb_recv, kv_send, kv_recv, part_send, part_recv,
    pair_send, pair_recv, z_send, z_recv, xs_send, xs_recv, ys_send, ys_recv,
    x2_send, x2_recv, y2_send, y2_recv, out_sem,
):
    dp = lax.axis_index("dp")
    p = lax.axis_index("pipe")
    s = lax.axis_index("seq")
    core = lax.rem(dp, 2)
    y_lo = dp // 2
    y_hi = s // 4
    x_at = lax.rem(s, 4)
    y_at = y_hi * 2 + y_lo

    def chip(x, y):
        return (lax.rem(y, 2) * 2 + core, p, (y // 2) * 4 + x)

    def along_x(step):
        return chip(lax.rem(x_at + step, 4), y_at)

    def along_y(step):
        return chip(x_at, lax.rem(y_at + step, 4))

    partner = (y_lo * 2 + 1 - core, p, s)

    def kv_copies():
        for half in range(2):
            for head in range(KVH):
                for which, ref in ((0, k_hbm), (1, v_hbm)):
                    yield pltpu.make_async_copy(
                        ref.at[pl.ds(half * HALF, HALF), pl.ds(head * HD, HD)],
                        kv.at[half, head, which, 0],
                        kv_local.at[half, head, which],
                    )

    copies = list(kv_copies())
    for copy in copies:
        copy.start()
    loads = [
        pltpu.make_async_copy(source, target, in_sem.at[i])
        for i, (source, target) in enumerate(
            ((norm_hbm, norm_in), (seg_hbm, seg), (g_hbm, g), (o_hbm, o), (q_hbm, q), (wk_hbm, wk), (wv_hbm, wv))
        )
    ]
    for copy in loads[:5]:
        copy.start()

    def x_columns(block, owner_core):
        y = lax.rem(y_at + block // 4, 4)
        x = lax.rem(x_at + block % 4, 4)
        row = (lax.rem(y, 2) * 2 + owner_core) * 1024 + (y // 2) * 512 + x * 128
        return pl.ds(pl.multiple_of(row, 128), 128)

    def xb_copy(block):
        return pltpu.make_async_copy(
            x_hbm.at[:, x_columns(block, core)], xb.at[0, :, pl.ds(block * 128, 128)], xb_local.at[block]
        )

    def xb_remote(block):
        return pltpu.make_async_remote_copy(
            src_ref=x_hbm.at[:, x_columns(block, 1 - core)],
            dst_ref=xb.at[1, :, pl.ds(block * 128, 128)],
            send_sem=xb_send.at[block],
            recv_sem=xb_recv.at[block],
            device_id=partner,
            device_id_type=MESH,
        )

    def in_row(step):
        return (dp, p, y_hi * 4 + lax.rem(x_at + step, 4))

    def kv_remote(dist, half, head, which=0, source=0):
        return pltpu.make_async_remote_copy(
            src_ref=kv.at[half, head, which, source],
            dst_ref=kv.at[half, head, which, dist],
            send_sem=kv_send.at[which, dist - 1, half, head],
            recv_sem=kv_recv.at[which, dist - 1, half, head],
            device_id=in_row(dist) if dist < NEAR and which == 0 else (dp, p, lax.rem(s + dist, 8)),
            device_id_type=MESH,
        )

    def part_remote(dist, half, head, which=0):
        return pltpu.make_async_remote_copy(
            src_ref=part_out.at[half, head, dist - 1, which],
            dst_ref=part_in.at[half, head, dist - 1, which],
            send_sem=part_send.at[which, dist - 1, half, head],
            recv_sem=part_recv.at[which, dist - 1, half, head],
            device_id=in_row(4 - dist) if dist < NEAR and which == 0 else (dp, p, lax.rem(s + 8 - dist, 8)),
            device_id_type=MESH,
        )

    def pair_remote(half, head):
        return pltpu.make_async_remote_copy(
            src_ref=pair.at[head, 0, half],
            dst_ref=pair.at[head, 1, half],
            send_sem=pair_send.at[half, head],
            recv_sem=pair_recv.at[half, head],
            device_id=partner,
            device_id_type=MESH,
        )

    def z_remote(half, chunk, hop=0):
        rows = pl.ds(half * HALF, HALF)
        at = pl.ds(pl.multiple_of(chunk * 1024, 1024), 1024)
        if isinstance(chunk, int) and chunk == 3:
            source = (up.at[rows, at], z_pass.at[half, 0], z_pass.at[half, 1])[hop]
            target = (z_pass.at[half, 0], z_pass.at[half, 1], up_hbm.at[rows, at])[hop]
            to, number = lax.rem(p + 1, 4), 3 + hop
        else:
            source, target, to, number = up.at[rows, at], up_hbm.at[rows, at], lax.rem(p + 3, 4), chunk
        return pltpu.make_async_remote_copy(
            src_ref=source,
            dst_ref=target,
            send_sem=z_send.at[half, number],
            recv_sem=z_recv.at[half, number],
            device_id=(dp, to, s),
            device_id_type=MESH,
        )

    def pass_z(half, hop):
        @pl.when(p != hop)
        def _():
            z_remote(half, 3, hop - 1).wait_recv()
            z_remote(half, 3, hop).start()

    def spread(source, target, send, recv, reach, head, step):
        return pltpu.make_async_remote_copy(
            src_ref=source.at[head, step - 1],
            dst_ref=target.at[head, step - 1],
            send_sem=send.at[head, step - 1],
            recv_sem=recv.at[head, step - 1],
            device_id=reach(step),
            device_id_type=MESH,
        )

    x_first = functools.partial(spread, xs_out, xs_in, xs_send, xs_recv, along_x)
    y_first = functools.partial(spread, ys_out, ys_in, ys_send, ys_recv, along_y)
    x_second = functools.partial(spread, x2_out, x2_in, x2_send, x2_recv, along_y)
    y_second = functools.partial(spread, y2_out, y2_in, y2_send, y2_recv, along_x)

    barrier = pltpu.get_barrier_semaphore()
    peers = [(dp, p, lax.rem(s + i, 8)) for i in range(1, 8)]
    peers += [along_y(i) for i in range(1, 4)]
    peers += [partner, (dp, lax.rem(p + 1, 4), s), (dp, lax.rem(p + 3, 4), s)]
    for peer in peers:
        pl.semaphore_signal(barrier, inc=1, device_id=peer, device_id_type=MESH)
    for copy in copies:
        copy.wait()
    pl.semaphore_wait(barrier, len(peers))

    def send_kv(half, head):
        @pl.when(s < NEAR)
        def _():
            kv_remote(NEAR, half, head).start()

        for dist in range(1, NEAR):

            @pl.when(x_at + dist < 4)
            def _(dist=dist):
                kv_remote(dist, half, head).start()

        for dist in range(1, NEAR + 1):

            @pl.when(s + dist <= 7)
            def _(dist=dist):
                kv_remote(dist, half, head, 1).start()

    def pass_kv(half, head):
        @pl.when(s >= NEAR)
        def _():
            kv_remote(NEAR, half, head).wait_recv()
            for dist in range(1, NEAR):

                @pl.when(x_at + dist >= 4)
                def _(dist=dist):
                    kv_remote(dist, half, head, 0, NEAR).start()

    send_kv(0, 0)
    for half in range(2):
        for head in range(KVH):
            for dist in range(1, NEAR + 1):

                @pl.when(s < dist)
                def _(dist=dist, half=half, head=head):
                    kv[half, head, :, dist] = jnp.zeros((2, HALF, HD), BF)

    loads[0].wait()
    loads[1].wait()
    norm_rows = norm_in[...].astype(F32) * LOG2E
    for head in range(HQ):
        norm[head] = jnp.broadcast_to(norm_rows[head : head + 1], (8, TOK))

    row_seg = seg[:, pl.ds(pl.multiple_of(s * TOK, TOK), TOK)].astype(F32)
    row_seg = jnp.broadcast_to(row_seg, (HALF, TOK))
    row_number = lax.broadcasted_iota(jnp.int32, (HALF, TOK), 1)
    key_number = lax.broadcasted_iota(jnp.int32, (HALF, TOK), 0)

    def document_bias(dist, half):
        block = lax.rem(s + 8 - dist, 8)
        at = pl.multiple_of(block * TOK + half * HALF, HALF)
        key_seg = jnp.broadcast_to(seg[:, pl.ds(at, HALF)].astype(F32), (HALF, HALF)).T
        same = jnp.concatenate([key_seg, key_seg], axis=1) == row_seg
        reach = jnp.where(s >= dist, 0.0, MASKED).astype(F32)
        return jnp.where(same, 0.0, MASKED) + reach

    for half in range(2):
        causal = key_number + half * HALF <= row_number
        bias[half, 0:HALF] = jnp.where(causal, document_bias(0, half), MASKED)
        for dist in range(1, NEAR + 1):
            bias[half, dist * HALF : (dist + 1) * HALF] = document_bias(dist, half)

    loads[2].wait()
    loads[3].wait()
    ones = jnp.ones((8, HD), BF)

    def delta_head(head, carry):
        at = pl.ds(pl.multiple_of(head * HD, HD), HD)
        product = g[:, at].astype(F32) * o[:, at].astype(F32)
        high = product.astype(BF)
        rest = product - high.astype(F32)
        middle = rest.astype(BF)
        low = (rest - middle.astype(F32)).astype(BF)
        total = dot(ones, high, 1, 1) + dot(ones, middle, 1, 1) + dot(ones, low, 1, 1)
        delta[head] = total.astype(BF).astype(F32)
        return carry

    lax.fori_loop(0, HQ, delta_head, 0, unroll=4)
    send_kv(0, 1)
    pass_kv(0, 0)
    loads[4].wait()
    loads[5].start()
    loads[6].start()
    for block in range(16):
        xb_copy(block).start()
        xb_remote(block).start()

    def fill():
        return pltpu.make_async_copy(zeros, up_hbm, out_sem.at[3])

    @pl.when(p == 3)
    def _():
        zeros[...] = jnp.zeros((TOK, D), BF)
        fill().start()

    def pass_part(half, head):
        @pl.when(s >= NEAR)
        def _():
            for dist in range(1, NEAR):

                @pl.when(x_at + dist >= 4)
                def _(dist=dist):
                    part_remote(dist, half, head).wait_recv()
                    relay[half, head] += part_in[half, head, dist - 1, 0].astype(F32)

            part_out[half, head, NEAR - 1, 0] = relay[half, head].astype(BF)
            part_remote(NEAR, half, head).start()

    def finalize(half, head):
        for dist in range(1, NEAR + 1):

            @pl.when(x_at + dist < 4 if dist < NEAR else s < NEAR)
            def _(dist=dist):
                part_remote(dist, half, head).wait_recv()
                own[half, head, 0] += part_in[half, head, dist - 1, 0].astype(F32)

            @pl.when(s + dist <= 7)
            def _(dist=dist):
                part_remote(dist, half, head, 1).wait_recv()
                own[half, head, 1] += part_in[half, head, dist - 1, 1].astype(F32)

        total = own[half, head].astype(BF)
        at = pl.multiple_of(head * HD, HD)
        grads[half, :, pl.ds(at, HD)] = total[0]
        grads[half, :, pl.ds(pl.multiple_of(at + KVH * HD, HD), HD)] = total[1]
        pair[head, 0, half, :, 0:HD] = total[0]
        pair[head, 0, half, :, HD : 2 * HD] = total[1]
        pair_remote(half, head).start()

    def input_grad(half):
        if half == 0:
            loads[5].wait()
            loads[6].wait()
        rows = pl.ds(half * HALF, HALF)

        def columns(chunk):
            for part in range(2):
                at = pl.ds(pl.multiple_of(chunk * 1024 + part * 512, 512), 512)
                total = dot(grads[half, :, 0 : KVH * HD], wk[at, :], 1, 1)
                total = total + dot(grads[half, :, KVH * HD : 2 * KVH * HD], wv[at, :], 1, 1)
                up[rows, at] = total.astype(BF)

            @pl.when(p > 0)
            def _():
                z_remote(half, chunk).start()

        def chunk_step(chunk, carry):
            columns(chunk)
            return carry

        columns(3)
        lax.fori_loop(0, 3, chunk_step, 0)

    def weight_terms(head):
        pair_remote(0, head).wait_recv()
        pair_remote(1, head).wait_recv()
        both = pair[head].reshape(2 * TOK, 2 * HD)

        def row_of_targets(ry):
            at = pl.ds(ry * 512, 512)
            terms = dot(both, xb[:, :, at].reshape(2 * TOK, 512), 0, 0)
            x_own[head, ry] = terms[0:HD, 0:HD]
            for rx in range(1, 4):
                xs_out[head, rx - 1, ry] = terms[0:HD, rx * HD : (rx + 1) * HD].astype(BF)
            for rx in range(4):
                if ry == 0:
                    y_own[head, rx] = terms[HD : 2 * HD, rx * HD : (rx + 1) * HD]
                else:
                    ys_out[head, ry - 1, rx] = terms[HD : 2 * HD, rx * HD : (rx + 1) * HD].astype(BF)

        for ry in range(4):
            row_of_targets(ry)
        for step in range(1, 4):
            x_first(head, step).start()
            y_first(head, step).start()

    def weight_sums(head):
        for step in range(1, 4):
            x_first(head, step).wait_recv()
            y_first(head, step).wait_recv()
        for r in range(4):
            total = x_own[head, r]
            other = y_own[head, r]
            for step in range(3):
                total = total + xs_in[head, step, r].astype(F32)
                other = other + ys_in[head, step, r].astype(F32)
            if r == 0:
                x_fin[head] = total
                y_fin[head] = other
            else:
                x2_out[head, r - 1] = total.astype(BF)
                y2_out[head, r - 1] = other.astype(BF)
        for step in range(1, 4):
            x_second(head, step).start()
            y_second(head, step).start()

    def weight_final(head):
        for step in range(1, 4):
            x_second(head, step).wait_recv()
            y_second(head, step).wait_recv()
        total = x_fin[head]
        other = y_fin[head]
        for step in range(3):
            total = total + x2_in[head, step].astype(F32)
            other = other + y2_in[head, step].astype(F32)
        at = pl.ds(pl.multiple_of(head * HD, HD), HD)
        gk[:, at] = total.T
        gv[:, at] = other.T

    def attend(half, head):
        for dist in range(1, NEAR):

            @pl.when(s >= dist)
            def _(dist=dist):
                kv_remote(dist, half, head).wait_recv()

        for dist in range(1, NEAR + 1):

            @pl.when(s >= dist)
            def _(dist=dist):
                kv_remote(dist, half, head, 1).wait_recv()

        keys = kv[half, head, 0].reshape((NEAR + 1) * HALF, HD)
        values = kv[half, head, 1].reshape((NEAR + 1) * HALF, HD)
        keys_t = keys.T
        total_k = jnp.zeros(((NEAR + 1) * HALF, HD), F32)
        total_v = jnp.zeros(((NEAR + 1) * HALF, HD), F32)
        for i in range(GROUP):
            at = pl.ds(pl.multiple_of(head * (GROUP * HD) + i * HD, HD), HD)
            q_head = q[:, at]
            g_head = g[:, at]
            number = head * GROUP + i
            scores = dot(keys, q_head, 1, 1)
            prob = jnp.exp2(scores * (SCALE * LOG2E) - norm[number][0:1] + bias[half])
            grad_prob = dot(values, g_head, 1, 1)
            grad_score = (prob * (grad_prob - delta[number][0:1])).astype(BF)
            total_v = total_v + dot(prob.astype(BF), g_head, 1, 0)
            total_k = total_k + dot(grad_score, q_head, 1, 0)
            grad_q = dot(keys_t, grad_score, 1, 0)
            if half == 0:
                dqt[number] = grad_q
            else:
                dq[:, at] = ((dqt[number] + grad_q) * SCALE).T.astype(BF)
        total_k = total_k * SCALE
        own[half, head, 0] = total_k[0:HALF]
        own[half, head, 1] = total_v[0:HALF]
        relay[half, head] = total_k[NEAR * HALF :]
        for dist in range(1, NEAR + 1):
            rows = slice(dist * HALF, (dist + 1) * HALF)
            if dist < NEAR:
                part_out[half, head, dist - 1, 0] = total_k[rows].astype(BF)
            part_out[half, head, dist - 1, 1] = total_v[rows].astype(BF)

            @pl.when(s >= dist)
            def _(dist=dist):
                if dist < NEAR:
                    part_remote(dist, half, head).start()
                part_remote(dist, half, head, 1).start()

    def first_half(head, carry):
        @pl.when(head < 2)
        def _():
            send_kv(0, head + 2)

        @pl.when(head >= 2)
        def _():
            send_kv(1, head - 2)
            pass_part(0, head - 2)

        @pl.when(head < 3)
        def _():
            pass_kv(0, head + 1)

        @pl.when(head == 3)
        def _():
            pass_kv(1, 0)
            finalize(0, 0)

        attend(0, head)
        return carry

    lax.fori_loop(0, KVH, first_half, 0)

    for block in range(16):
        xb_copy(block).wait()
        xb_remote(block).wait_recv()

    def second_half(head, carry):
        @pl.when(head < 2)
        def _():
            send_kv(1, head + 2)
            pass_part(0, head + 2)

        @pl.when(head >= 2)
        def _():
            pass_part(1, head - 2)

        @pl.when(head < 3)
        def _():
            pass_kv(1, head + 1)
            finalize(0, head + 1)

        @pl.when(head == 2)
        def _():
            input_grad(0)

        @pl.when(head == 3)
        def _():
            finalize(1, 0)

        attend(1, head)
        return carry

    lax.fori_loop(0, KVH, second_half, 0)
    store_dq = pltpu.make_async_copy(dq, dq_hbm, out_sem.at[0])
    store_dq.start()
    pass_part(1, 2)
    pass_z(0, 1)
    finalize(1, 1)
    weight_terms(0)
    pass_part(1, 3)
    finalize(1, 2)
    weight_terms(1)
    finalize(1, 3)
    input_grad(1)
    pass_z(0, 2)
    weight_terms(2)
    weight_terms(3)
    weight_sums(0)
    weight_sums(1)
    pass_z(1, 1)
    weight_sums(2)
    weight_sums(3)

    def finish(head, carry):
        weight_final(head)
        return carry

    lax.fori_loop(0, KVH, finish, 0)
    store_gk = pltpu.make_async_copy(gk, gk_hbm, out_sem.at[1])
    store_gv = pltpu.make_async_copy(gv, gv_hbm, out_sem.at[2])
    store_gk.start()
    store_gv.start()
    pass_z(1, 2)

    for half in range(2):

        def sent(head, carry, half=half):
            for dist in range(1, NEAR):

                @pl.when(jnp.logical_or(x_at + dist < 4, s >= NEAR))
                def _(dist=dist):
                    kv_remote(dist, half, head).wait_send()

                @pl.when(s >= dist)
                def _(dist=dist):
                    part_remote(dist, half, head).wait_send()

            for dist in range(1, NEAR + 1):

                @pl.when(s + dist <= 7)
                def _(dist=dist):
                    kv_remote(dist, half, head, 1).wait_send()

                @pl.when(s >= dist)
                def _(dist=dist):
                    part_remote(dist, half, head, 1).wait_send()

            @pl.when(s < NEAR)
            def _():
                kv_remote(NEAR, half, head).wait_send()

            @pl.when(s >= NEAR)
            def _():
                part_remote(NEAR, half, head).wait_send()

            pair_remote(half, head).wait_send()

            return carry

        lax.fori_loop(0, 4, sent, 0)

    def sums_sent(head, carry):
        for step in range(1, 4):
            x_first(head, step).wait_send()
            y_first(head, step).wait_send()
            x_second(head, step).wait_send()
            y_second(head, step).wait_send()
        return carry

    lax.fori_loop(0, KVH, sums_sent, 0)
    for half in range(2):

        @pl.when(p > 0)
        def _(half=half):
            for chunk in range(4):
                z_remote(half, chunk).wait_send()

        for hop in (1, 2):

            @pl.when(p != hop)
            def _(half=half, hop=hop):
                z_remote(half, 3, hop).wait_send()

        @pl.when(p < 3)
        def _(half=half):
            for chunk in range(3):
                z_remote(half, chunk).wait_recv()
            z_remote(half, 3, 2).wait_recv()

    for block in range(16):
        xb_remote(block).wait_send()

    @pl.when(p == 3)
    def _():
        fill().wait()

    store_dq.wait()
    store_gk.wait()
    store_gv.wait()


def hand_out(dq, up, gk, gv, dq_out, up_out, gk_out, gv_out):
    dq_out[...] = dq[...]
    up_out[...] = up[...]
    gk_out[...] = gk[...]
    gv_out[...] = gv[...]


def shards(
    layer_input, queries, keys, values, attn_out, out_grad, log_norm, segment_ids, key_weight, value_weight
):
    any_space = pl.BlockSpec(memory_space=pl.ANY)
    vmem = pltpu.VMEM
    dma = pltpu.SemaphoreType.DMA
    pieces = (2, KVH, NEAR, 2, HALF, HD)
    out_shape = (
        jax.ShapeDtypeStruct((TOK, D), BF),
        jax.ShapeDtypeStruct((TOK, D), BF),
        jax.ShapeDtypeStruct((128, KVH * HD), F32),
        jax.ShapeDtypeStruct((128, KVH * HD), F32),
    )
    outs = pl.pallas_call(
        kernel,
        out_shape=out_shape,
        in_specs=[any_space] * 10,
        out_specs=(any_space,) * 4,
        scratch_shapes=[
            vmem((TOK, D), BF),
            vmem((TOK, D), BF),
            vmem((TOK, D), BF),
            vmem((HQ, TOK), BF),
            vmem((1, 8 * TOK), jnp.int32),
            vmem((D, KVH * HD), BF),
            vmem((D, KVH * HD), BF),
            vmem((2, KVH, 2, NEAR + 1, HALF, HD), BF),
            vmem((HQ, 8, TOK), F32),
            vmem((HQ, 8, TOK), F32),
            vmem((2, (NEAR + 1) * HALF, TOK), F32),
            vmem((HQ, HD, TOK), F32),
            vmem((TOK, D), BF),
            vmem(pieces, BF),
            vmem(pieces, BF),
            vmem((2, KVH, HALF, HD), F32),
            vmem((2, KVH, 2, HALF, HD), F32),
            vmem((2, HALF, 2 * KVH * HD), BF),
            vmem((KVH, 2, 2, HALF, 2 * HD), BF),
            vmem((2, TOK, 2048), BF),
            vmem((TOK, D), BF),
            vmem((2, 2, HALF, 1024), BF),
            vmem((TOK, D), BF),
            vmem((KVH, 3, 4, HD, HD), BF),
            vmem((KVH, 3, 4, HD, HD), BF),
            vmem((KVH, 3, 4, HD, HD), BF),
            vmem((KVH, 3, 4, HD, HD), BF),
            vmem((KVH, 4, HD, HD), F32),
            vmem((KVH, 4, HD, HD), F32),
            vmem((KVH, 3, HD, HD), BF),
            vmem((KVH, 3, HD, HD), BF),
            vmem((KVH, 3, HD, HD), BF),
            vmem((KVH, 3, HD, HD), BF),
            vmem((KVH, HD, HD), F32),
            vmem((KVH, HD, HD), F32),
            vmem((128, KVH * HD), F32),
            vmem((128, KVH * HD), F32),
            dma((7,)),
            dma((2, KVH, 2)),
            dma((16,)),
            dma((16,)),
            dma((16,)),
            dma((2, NEAR, 2, KVH)),
            dma((2, NEAR, 2, KVH)),
            dma((2, NEAR, 2, KVH)),
            dma((2, NEAR, 2, KVH)),
            dma((2, KVH)),
            dma((2, KVH)),
            dma((2, 6)),
            dma((2, 6)),
        ]
        + [dma((KVH, 3))] * 8
        + [dma((4,))],
        compiler_params=pltpu.CompilerParams(
            collective_id=0, has_side_effects=True, vmem_limit_bytes=60 * 1024 * 1024
        ),
        cost_estimate=pl.CostEstimate(flops=20_000_000_000, bytes_accessed=24_000_000, transcendentals=8_000_000),
        name="attention_backward",
    )(
        layer_input[0, 0], queries[0, 0], keys[0, 0], values[0, 0], attn_out[0, 0], out_grad[0, 0],
        log_norm[0, 0].T, segment_ids[0], key_weight[0], value_weight[0],
    )
    blocks = tuple(pl.BlockSpec((rows // 2, columns), lambda i: (i, 0)) for rows, columns in (o.shape for o in out_shape))
    query_grad, upstream, grad_wk, grad_wv = pl.pallas_call(
        hand_out,
        out_shape=out_shape,
        grid=(2,),
        in_specs=blocks,
        out_specs=blocks,
        name="hand_out",
    )(*outs)
    return (query_grad[None, None], upstream[None, None], grad_wk[None], grad_wv[None])


def solution(mesh):
    rows = P("dp", "pipe", "seq", None)
    weight = P("pipe", None, None)
    return jax.shard_map(
        shards,
        mesh=mesh,
        in_specs=(rows,) * 7 + (P("dp", "pipe", None), weight, weight),
        out_specs=(rows, rows, P("pipe", ("dp", "seq"), None), P("pipe", ("dp", "seq"), None)),
        check_vma=False,
    )
```

```python
import functools
import math

import jax
import jax.numpy as jnp
from jax import lax
from jax.experimental import pallas as pl
from jax.experimental.pallas import tpu as pltpu
from jax.sharding import PartitionSpec as P

HQ = 32
KVH = 4
GROUP = HQ // KVH
HD = 128
TOK = 256
HALF = 128
D = 4096
NEAR = 4
SCALE = 1.0 / math.sqrt(HD)
LOG2E = math.log2(math.e)
MASKED = -1e30
MESH = pl.DeviceIdType.MESH
BF = jnp.bfloat16
F32 = jnp.float32


def dot(a, b, ca, cb):
    return lax.dot_general(a, b, (((ca,), (cb,)), ((), ())), preferred_element_type=F32)


def kernel(
    x_hbm, q_hbm, k_hbm, v_hbm, o_hbm, g_hbm, norm_hbm, seg_hbm, wk_hbm, wv_hbm,
    dq_hbm, up_hbm, gk_hbm, gv_hbm,
    q, g, o, norm_in, seg, wk, wv, kv, norm, delta, bias, dqt, dq,
    part_out, part_in, relay, own, grads, pair, xb, up, z_pass, zeros,
    xs_out, xs_in, ys_out, ys_in, x_own, y_own, x2_out, x2_in, y2_out, y2_in, x_fin, y_fin, gk, gv,
    in_sem, kv_local, xb_local, xb_send, xb_recv, kv_send, kv_recv, part_send, part_recv,
    pair_send, pair_recv, z_send, z_recv, xs_send, xs_recv, ys_send, ys_recv,
    x2_send, x2_recv, y2_send, y2_recv, out_sem,
):
    dp = lax.axis_index("dp")
    p = lax.axis_index("pipe")
    s = lax.axis_index("seq")
    core = lax.rem(dp, 2)
    y_lo = dp // 2
    y_hi = s // 4
    x_at = lax.rem(s, 4)
    y_at = y_hi * 2 + y_lo

    def chip(x, y):
        return (lax.rem(y, 2) * 2 + core, p, (y // 2) * 4 + x)

    def along_x(step):
        return chip(lax.rem(x_at + step, 4), y_at)

    def along_y(step):
        return chip(x_at, lax.rem(y_at + step, 4))

    partner = (y_lo * 2 + 1 - core, p, s)

    def kv_copies():
        for half in range(2):
            for head in range(KVH):
                for which, ref in ((0, k_hbm), (1, v_hbm)):
                    yield pltpu.make_async_copy(
                        ref.at[pl.ds(half * HALF, HALF), pl.ds(head * HD, HD)],
                        kv.at[half, head, which, 0],
                        kv_local.at[half, head, which],
                    )

    copies = list(kv_copies())
    for copy in copies:
        copy.start()
    loads = [
        pltpu.make_async_copy(source, target, in_sem.at[i])
        for i, (source, target) in enumerate(
            ((norm_hbm, norm_in), (seg_hbm, seg), (g_hbm, g), (o_hbm, o), (q_hbm, q), (wk_hbm, wk), (wv_hbm, wv))
        )
    ]
    for copy in loads[:5]:
        copy.start()

    def x_columns(block, owner_core):
        y = lax.rem(y_at + block // 4, 4)
        x = lax.rem(x_at + block % 4, 4)
        row = (lax.rem(y, 2) * 2 + owner_core) * 1024 + (y // 2) * 512 + x * 128
        return pl.ds(pl.multiple_of(row, 128), 128)

    def xb_copy(block):
        return pltpu.make_async_copy(
            x_hbm.at[:, x_columns(block, core)], xb.at[0, :, pl.ds(block * 128, 128)], xb_local.at[block]
        )

    def xb_remote(block):
        return pltpu.make_async_remote_copy(
            src_ref=x_hbm.at[:, x_columns(block, 1 - core)],
            dst_ref=xb.at[1, :, pl.ds(block * 128, 128)],
            send_sem=xb_send.at[block],
            recv_sem=xb_recv.at[block],
            device_id=partner,
            device_id_type=MESH,
        )

    def in_row(step):
        return (dp, p, y_hi * 4 + lax.rem(x_at + step, 4))

    def kv_remote(dist, half, head, which=0, source=0):
        return pltpu.make_async_remote_copy(
            src_ref=kv.at[half, head, which, source],
            dst_ref=kv.at[half, head, which, dist],
            send_sem=kv_send.at[which, dist - 1, half, head],
            recv_sem=kv_recv.at[which, dist - 1, half, head],
            device_id=in_row(dist) if dist < NEAR and which == 0 else (dp, p, lax.rem(s + dist, 8)),
            device_id_type=MESH,
        )

    def part_remote(dist, half, head, which=0):
        return pltpu.make_async_remote_copy(
            src_ref=part_out.at[half, head, dist - 1, which],
            dst_ref=part_in.at[half, head, dist - 1, which],
            send_sem=part_send.at[which, dist - 1, half, head],
            recv_sem=part_recv.at[which, dist - 1, half, head],
            device_id=in_row(4 - dist) if dist < NEAR and which == 0 else (dp, p, lax.rem(s + 8 - dist, 8)),
            device_id_type=MESH,
        )

    def pair_remote(half, head):
        return pltpu.make_async_remote_copy(
            src_ref=pair.at[head, 0, half],
            dst_ref=pair.at[head, 1, half],
            send_sem=pair_send.at[half, head],
            recv_sem=pair_recv.at[half, head],
            device_id=partner,
            device_id_type=MESH,
        )

    def z_remote(half, chunk, hop=0):
        rows = pl.ds(half * HALF, HALF)
        at = pl.ds(pl.multiple_of(chunk * 1024, 1024), 1024)
        if isinstance(chunk, int) and chunk == 3:
            source = (up.at[rows, at], z_pass.at[half, 0], z_pass.at[half, 1])[hop]
            target = (z_pass.at[half, 0], z_pass.at[half, 1], up_hbm.at[rows, at])[hop]
            to, number = lax.rem(p + 1, 4), 3 + hop
        else:
            source, target, to, number = up.at[rows, at], up_hbm.at[rows, at], lax.rem(p + 3, 4), chunk
        return pltpu.make_async_remote_copy(
            src_ref=source,
            dst_ref=target,
            send_sem=z_send.at[half, number],
            recv_sem=z_recv.at[half, number],
            device_id=(dp, to, s),
            device_id_type=MESH,
        )

    def pass_z(half, hop):
        @pl.when(p != hop)
        def _():
            z_remote(half, 3, hop - 1).wait_recv()
            z_remote(half, 3, hop).start()

    def spread(source, target, send, recv, reach, head, step):
        return pltpu.make_async_remote_copy(
            src_ref=source.at[head, step - 1],
            dst_ref=target.at[head, step - 1],
            send_sem=send.at[head, step - 1],
            recv_sem=recv.at[head, step - 1],
            device_id=reach(step),
            device_id_type=MESH,
        )

    x_first = functools.partial(spread, xs_out, xs_in, xs_send, xs_recv, along_x)
    y_first = functools.partial(spread, ys_out, ys_in, ys_send, ys_recv, along_y)
    x_second = functools.partial(spread, x2_out, x2_in, x2_send, x2_recv, along_y)
    y_second = functools.partial(spread, y2_out, y2_in, y2_send, y2_recv, along_x)

    barrier = pltpu.get_barrier_semaphore()
    peers = [(dp, p, lax.rem(s + i, 8)) for i in range(1, 8)]
    peers += [along_y(i) for i in range(1, 4)]
    peers += [partner, (dp, lax.rem(p + 1, 4), s), (dp, lax.rem(p + 3, 4), s)]
    for peer in peers:
        pl.semaphore_signal(barrier, inc=1, device_id=peer, device_id_type=MESH)
    for copy in copies:
        copy.wait()
    pl.semaphore_wait(barrier, len(peers))

    def send_kv(half, head):
        @pl.when(s < NEAR)
        def _():
            kv_remote(NEAR, half, head).start()

        for dist in range(1, NEAR):

            @pl.when(x_at + dist < 4)
            def _(dist=dist):
                kv_remote(dist, half, head).start()

        for dist in range(1, NEAR + 1):

            @pl.when(s + dist <= 7)
            def _(dist=dist):
                kv_remote(dist, half, head, 1).start()

    def pass_kv(half, head):
        @pl.when(s >= NEAR)
        def _():
            kv_remote(NEAR, half, head).wait_recv()
            for dist in range(1, NEAR):

                @pl.when(x_at + dist >= 4)
                def _(dist=dist):
                    kv_remote(dist, half, head, 0, NEAR).start()

    send_kv(0, 0)
    for half in range(2):
        for head in range(KVH):
            for dist in range(1, NEAR + 1):

                @pl.when(s < dist)
                def _(dist=dist, half=half, head=head):
                    kv[half, head, :, dist] = jnp.zeros((2, HALF, HD), BF)

    loads[0].wait()
    loads[1].wait()
    norm_rows = norm_in[...].astype(F32) * LOG2E
    for head in range(HQ):
        norm[head] = jnp.broadcast_to(norm_rows[head : head + 1], (8, TOK))

    row_seg = seg[:, pl.ds(pl.multiple_of(s * TOK, TOK), TOK)].astype(F32)
    row_seg = jnp.broadcast_to(row_seg, (HALF, TOK))
    row_number = lax.broadcasted_iota(jnp.int32, (HALF, TOK), 1)
    key_number = lax.broadcasted_iota(jnp.int32, (HALF, TOK), 0)

    def document_bias(dist, half):
        block = lax.rem(s + 8 - dist, 8)
        at = pl.multiple_of(block * TOK + half * HALF, HALF)
        key_seg = jnp.broadcast_to(seg[:, pl.ds(at, HALF)].astype(F32), (HALF, HALF)).T
        same = jnp.concatenate([key_seg, key_seg], axis=1) == row_seg
        reach = jnp.where(s >= dist, 0.0, MASKED).astype(F32)
        return jnp.where(same, 0.0, MASKED) + reach

    for half in range(2):
        causal = key_number + half * HALF <= row_number
        bias[half, 0:HALF] = jnp.where(causal, document_bias(0, half), MASKED)
        for dist in range(1, NEAR + 1):
            bias[half, dist * HALF : (dist + 1) * HALF] = document_bias(dist, half)

    loads[2].wait()
    loads[3].wait()
    ones = jnp.ones((8, HD), BF)

    def delta_head(head, carry):
        at = pl.ds(pl.multiple_of(head * HD, HD), HD)
        product = g[:, at].astype(F32) * o[:, at].astype(F32)
        high = product.astype(BF)
        rest = product - high.astype(F32)
        middle = rest.astype(BF)
        low = (rest - middle.astype(F32)).astype(BF)
        total = dot(ones, high, 1, 1) + dot(ones, middle, 1, 1) + dot(ones, low, 1, 1)
        delta[head] = total.astype(BF).astype(F32)
        return carry

    lax.fori_loop(0, HQ, delta_head, 0, unroll=4)
    send_kv(0, 1)
    pass_kv(0, 0)
    send_kv(0, 2)
    loads[4].wait()
    loads[5].start()
    loads[6].start()
    for block in range(16):
        xb_copy(block).start()
        xb_remote(block).start()

    def fill():
        return pltpu.make_async_copy(zeros, up_hbm, out_sem.at[3])

    @pl.when(p == 3)
    def _():
        zeros[...] = jnp.zeros((TOK, D), BF)
        fill().start()

    def pass_part(half, head):
        @pl.when(s >= NEAR)
        def _():
            for dist in range(1, NEAR):

                @pl.when(x_at + dist >= 4)
                def _(dist=dist):
                    part_remote(dist, half, head).wait_recv()
                    relay[half, head] += part_in[half, head, dist - 1, 0].astype(F32)

            part_out[half, head, NEAR - 1, 0] = relay[half, head].astype(BF)
            part_remote(NEAR, half, head).start()

    def finalize(half, head):
        for dist in range(1, NEAR + 1):

            @pl.when(x_at + dist < 4 if dist < NEAR else s < NEAR)
            def _(dist=dist):
                part_remote(dist, half, head).wait_recv()
                own[half, head, 0] += part_in[half, head, dist - 1, 0].astype(F32)

            @pl.when(s + dist <= 7)
            def _(dist=dist):
                part_remote(dist, half, head, 1).wait_recv()
                own[half, head, 1] += part_in[half, head, dist - 1, 1].astype(F32)

        total = own[half, head].astype(BF)
        at = pl.multiple_of(head * HD, HD)
        grads[half, :, pl.ds(at, HD)] = total[0]
        grads[half, :, pl.ds(pl.multiple_of(at + KVH * HD, HD), HD)] = total[1]
        pair[head, 0, half, :, 0:HD] = total[0]
        pair[head, 0, half, :, HD : 2 * HD] = total[1]
        pair_remote(half, head).start()

    def input_grad(half):
        if half == 0:
            loads[5].wait()
            loads[6].wait()
        rows = pl.ds(half * HALF, HALF)

        def columns(chunk):
            for part in range(2):
                at = pl.ds(pl.multiple_of(chunk * 1024 + part * 512, 512), 512)
                total = dot(grads[half, :, 0 : KVH * HD], wk[at, :], 1, 1)
                total = total + dot(grads[half, :, KVH * HD : 2 * KVH * HD], wv[at, :], 1, 1)
                up[rows, at] = total.astype(BF)

            @pl.when(p > 0)
            def _():
                z_remote(half, chunk).start()

        def chunk_step(chunk, carry):
            columns(chunk)
            return carry

        columns(3)
        lax.fori_loop(0, 3, chunk_step, 0)

    def weight_terms(head):
        pair_remote(0, head).wait_recv()
        pair_remote(1, head).wait_recv()
        both = pair[head].reshape(2 * TOK, 2 * HD)

        def row_of_targets(ry):
            at = pl.ds(ry * 512, 512)
            terms = dot(both, xb[:, :, at].reshape(2 * TOK, 512), 0, 0)
            x_own[head, ry] = terms[0:HD, 0:HD]
            for rx in range(1, 4):
                xs_out[head, rx - 1, ry] = terms[0:HD, rx * HD : (rx + 1) * HD].astype(BF)
            for rx in range(4):
                if ry == 0:
                    y_own[head, rx] = terms[HD : 2 * HD, rx * HD : (rx + 1) * HD]
                else:
                    ys_out[head, ry - 1, rx] = terms[HD : 2 * HD, rx * HD : (rx + 1) * HD].astype(BF)

        for ry in range(4):
            row_of_targets(ry)
            if ry > 0:
                y_first(head, ry).start()
        for step in range(1, 4):
            x_first(head, step).start()

    def weight_sums(head):
        for step in range(1, 4):
            x_first(head, step).wait_recv()
            y_first(head, step).wait_recv()
        for r in range(4):
            total = x_own[head, r]
            other = y_own[head, r]
            for step in range(3):
                total = total + xs_in[head, step, r].astype(F32)
                other = other + ys_in[head, step, r].astype(F32)
            if r == 0:
                x_fin[head] = total
                y_fin[head] = other
            else:
                x2_out[head, r - 1] = total.astype(BF)
                y2_out[head, r - 1] = other.astype(BF)
        for step in range(1, 4):
            x_second(head, step).start()
            y_second(head, step).start()

    def weight_final(head):
        for step in range(1, 4):
            x_second(head, step).wait_recv()
            y_second(head, step).wait_recv()
        total = x_fin[head]
        other = y_fin[head]
        for step in range(3):
            total = total + x2_in[head, step].astype(F32)
            other = other + y2_in[head, step].astype(F32)
        at = pl.ds(pl.multiple_of(head * HD, HD), HD)
        gk[:, at] = total.T
        gv[:, at] = other.T

    def attend(half, head):
        for dist in range(1, NEAR):

            @pl.when(s >= dist)
            def _(dist=dist):
                kv_remote(dist, half, head).wait_recv()

        for dist in range(1, NEAR + 1):

            @pl.when(s >= dist)
            def _(dist=dist):
                kv_remote(dist, half, head, 1).wait_recv()

        keys = kv[half, head, 0].reshape((NEAR + 1) * HALF, HD)
        values = kv[half, head, 1].reshape((NEAR + 1) * HALF, HD)
        keys_t = keys.T
        total_k = jnp.zeros(((NEAR + 1) * HALF, HD), F32)
        total_v = jnp.zeros(((NEAR + 1) * HALF, HD), F32)
        for i in range(GROUP):
            at = pl.ds(pl.multiple_of(head * (GROUP * HD) + i * HD, HD), HD)
            q_head = q[:, at]
            g_head = g[:, at]
            number = head * GROUP + i
            scores = dot(keys, q_head, 1, 1)
            prob = jnp.exp2(scores * (SCALE * LOG2E) - norm[number][0:1] + bias[half])
            grad_prob = dot(values, g_head, 1, 1)
            grad_score = (prob * (grad_prob - delta[number][0:1])).astype(BF)
            total_v = total_v + dot(prob.astype(BF), g_head, 1, 0)
            total_k = total_k + dot(grad_score, q_head, 1, 0)
            grad_q = dot(keys_t, grad_score, 1, 0)
            if half == 0:
                dqt[number] = grad_q
            else:
                dq[:, at] = ((dqt[number] + grad_q) * SCALE).T.astype(BF)
        total_k = total_k * SCALE
        own[half, head, 0] = total_k[0:HALF]
        own[half, head, 1] = total_v[0:HALF]
        relay[half, head] = total_k[NEAR * HALF :]
        for dist in range(1, NEAR + 1):
            rows = slice(dist * HALF, (dist + 1) * HALF)
            if dist < NEAR:
                part_out[half, head, dist - 1, 0] = total_k[rows].astype(BF)
            part_out[half, head, dist - 1, 1] = total_v[rows].astype(BF)

            @pl.when(s >= dist)
            def _(dist=dist):
                if dist < NEAR:
                    part_remote(dist, half, head).start()
                part_remote(dist, half, head, 1).start()

    def first_half(head, carry):
        @pl.when(head == 0)
        def _():
            send_kv(0, 3)

        @pl.when(head > 0)
        def _():
            send_kv(1, head - 1)

        @pl.when(head >= 2)
        def _():
            pass_part(0, head - 2)

        @pl.when(head < 3)
        def _():
            pass_kv(0, head + 1)

        @pl.when(head == 3)
        def _():
            pass_kv(1, 0)
            finalize(0, 0)

        attend(0, head)
        return carry

    lax.fori_loop(0, KVH, first_half, 0)

    for block in range(16):
        xb_copy(block).wait()
        xb_remote(block).wait_recv()

    def second_half(head, carry):
        @pl.when(head == 0)
        def _():
            send_kv(1, 3)

        @pl.when(head < 2)
        def _():
            pass_part(0, head + 2)

        @pl.when(head >= 2)
        def _():
            pass_part(1, head - 2)

        @pl.when(head < 3)
        def _():
            pass_kv(1, head + 1)
            finalize(0, head + 1)

        @pl.when(head == 2)
        def _():
            input_grad(0)

        @pl.when(head == 3)
        def _():
            finalize(1, 0)

        attend(1, head)
        return carry

    lax.fori_loop(0, KVH, second_half, 0)
    store_dq = pltpu.make_async_copy(dq, dq_hbm, out_sem.at[0])
    store_dq.start()
    pass_part(1, 2)
    finalize(1, 1)
    weight_terms(0)
    pass_z(0, 1)
    pass_part(1, 3)
    finalize(1, 2)
    weight_terms(1)
    finalize(1, 3)
    input_grad(1)
    weight_terms(2)
    weight_terms(3)
    pass_z(0, 2)
    weight_sums(0)
    pass_z(1, 1)
    weight_sums(1)
    weight_sums(2)
    pass_z(1, 2)
    weight_sums(3)

    def finish(head, carry):
        weight_final(head)
        return carry

    lax.fori_loop(0, KVH, finish, 0)
    store_gk = pltpu.make_async_copy(gk, gk_hbm, out_sem.at[1])
    store_gv = pltpu.make_async_copy(gv, gv_hbm, out_sem.at[2])
    store_gk.start()
    store_gv.start()

    for half in range(2):

        def sent(head, carry, half=half):
            for dist in range(1, NEAR):

                @pl.when(jnp.logical_or(x_at + dist < 4, s >= NEAR))
                def _(dist=dist):
                    kv_remote(dist, half, head).wait_send()

                @pl.when(s >= dist)
                def _(dist=dist):
                    part_remote(dist, half, head).wait_send()

            for dist in range(1, NEAR + 1):

                @pl.when(s + dist <= 7)
                def _(dist=dist):
                    kv_remote(dist, half, head, 1).wait_send()

                @pl.when(s >= dist)
                def _(dist=dist):
                    part_remote(dist, half, head, 1).wait_send()

            @pl.when(s < NEAR)
            def _():
                kv_remote(NEAR, half, head).wait_send()

            @pl.when(s >= NEAR)
            def _():
                part_remote(NEAR, half, head).wait_send()

            pair_remote(half, head).wait_send()

            return carry

        lax.fori_loop(0, 4, sent, 0)

    def sums_sent(head, carry):
        for step in range(1, 4):
            x_first(head, step).wait_send()
            y_first(head, step).wait_send()
            x_second(head, step).wait_send()
            y_second(head, step).wait_send()
        return carry

    lax.fori_loop(0, KVH, sums_sent, 0)
    for half in range(2):

        @pl.when(p > 0)
        def _(half=half):
            for chunk in range(4):
                z_remote(half, chunk).wait_send()

        for hop in (1, 2):

            @pl.when(p != hop)
            def _(half=half, hop=hop):
                z_remote(half, 3, hop).wait_send()

        @pl.when(p < 3)
        def _(half=half):
            for chunk in range(3):
                z_remote(half, chunk).wait_recv()
            z_remote(half, 3, 2).wait_recv()

    for block in range(16):
        xb_remote(block).wait_send()

    @pl.when(p == 3)
    def _():
        fill().wait()

    store_dq.wait()
    store_gk.wait()
    store_gv.wait()


def hand_out(dq, up, gk, gv, dq_out, up_out, gk_out, gv_out, dq_held, up_held, gk_held, gv_held, into, out):
    pieces = []
    for source, held, target, parts in (
        (dq, dq_held, dq_out, 4), (up, up_held, up_out, 4), (gk, gk_held, gk_out, 1), (gv, gv_held, gv_out, 1)
    ):
        size = source.shape[0] // parts
        for part in range(parts):
            rows = pl.ds(part * size, size)
            number = len(pieces)
            pieces.append((
                pltpu.make_async_copy(source.at[rows], held.at[rows], into.at[number]),
                pltpu.make_async_copy(held.at[rows], target.at[rows], out.at[number]),
            ))
    for first, _ in pieces:
        first.start()
    for first, second in pieces:
        first.wait()
        second.start()
    for _, second in pieces:
        second.wait()


def shards(
    layer_input, queries, keys, values, attn_out, out_grad, log_norm, segment_ids, key_weight, value_weight
):
    any_space = pl.BlockSpec(memory_space=pl.ANY)
    vmem = pltpu.VMEM
    dma = pltpu.SemaphoreType.DMA
    pieces = (2, KVH, NEAR, 2, HALF, HD)
    out_shape = (
        jax.ShapeDtypeStruct((TOK, D), BF),
        jax.ShapeDtypeStruct((TOK, D), BF),
        jax.ShapeDtypeStruct((128, KVH * HD), F32),
        jax.ShapeDtypeStruct((128, KVH * HD), F32),
    )
    outs = pl.pallas_call(
        kernel,
        out_shape=out_shape,
        in_specs=[any_space] * 10,
        out_specs=(any_space,) * 4,
        scratch_shapes=[
            vmem((TOK, D), BF),
            vmem((TOK, D), BF),
            vmem((TOK, D), BF),
            vmem((HQ, TOK), BF),
            vmem((1, 8 * TOK), jnp.int32),
            vmem((D, KVH * HD), BF),
            vmem((D, KVH * HD), BF),
            vmem((2, KVH, 2, NEAR + 1, HALF, HD), BF),
            vmem((HQ, 8, TOK), F32),
            vmem((HQ, 8, TOK), F32),
            vmem((2, (NEAR + 1) * HALF, TOK), F32),
            vmem((HQ, HD, TOK), F32),
            vmem((TOK, D), BF),
            vmem(pieces, BF),
            vmem(pieces, BF),
            vmem((2, KVH, HALF, HD), F32),
            vmem((2, KVH, 2, HALF, HD), F32),
            vmem((2, HALF, 2 * KVH * HD), BF),
            vmem((KVH, 2, 2, HALF, 2 * HD), BF),
            vmem((2, TOK, 2048), BF),
            vmem((TOK, D), BF),
            vmem((2, 2, HALF, 1024), BF),
            vmem((TOK, D), BF),
            vmem((KVH, 3, 4, HD, HD), BF),
            vmem((KVH, 3, 4, HD, HD), BF),
            vmem((KVH, 3, 4, HD, HD), BF),
            vmem((KVH, 3, 4, HD, HD), BF),
            vmem((KVH, 4, HD, HD), F32),
            vmem((KVH, 4, HD, HD), F32),
            vmem((KVH, 3, HD, HD), BF),
            vmem((KVH, 3, HD, HD), BF),
            vmem((KVH, 3, HD, HD), BF),
            vmem((KVH, 3, HD, HD), BF),
            vmem((KVH, HD, HD), F32),
            vmem((KVH, HD, HD), F32),
            vmem((128, KVH * HD), F32),
            vmem((128, KVH * HD), F32),
            dma((7,)),
            dma((2, KVH, 2)),
            dma((16,)),
            dma((16,)),
            dma((16,)),
            dma((2, NEAR, 2, KVH)),
            dma((2, NEAR, 2, KVH)),
            dma((2, NEAR, 2, KVH)),
            dma((2, NEAR, 2, KVH)),
            dma((2, KVH)),
            dma((2, KVH)),
            dma((2, 6)),
            dma((2, 6)),
        ]
        + [dma((KVH, 3))] * 8
        + [dma((4,))],
        compiler_params=pltpu.CompilerParams(
            collective_id=0, has_side_effects=True, vmem_limit_bytes=60 * 1024 * 1024
        ),
        cost_estimate=pl.CostEstimate(flops=20_000_000_000, bytes_accessed=24_000_000, transcendentals=8_000_000),
        name="attention_backward",
    )(
        layer_input[0, 0], queries[0, 0], keys[0, 0], values[0, 0], attn_out[0, 0], out_grad[0, 0],
        log_norm[0, 0].T, segment_ids[0], key_weight[0], value_weight[0],
    )
    query_grad, upstream, grad_wk, grad_wv = pl.pallas_call(
        hand_out,
        out_shape=out_shape,
        in_specs=[any_space] * 4,
        out_specs=(any_space,) * 4,
        scratch_shapes=[vmem(o.shape, o.dtype) for o in out_shape] + [dma((10,)), dma((10,))],
        name="hand_out",
    )(*outs)
    return (query_grad[None, None], upstream[None, None], grad_wk[None], grad_wv[None])


def solution(mesh):
    rows = P("dp", "pipe", "seq", None)
    weight = P("pipe", None, None)
    return jax.shard_map(
        shards,
        mesh=mesh,
        in_specs=(rows,) * 7 + (P("dp", "pipe", None), weight, weight),
        out_specs=(rows, rows, P("pipe", ("dp", "seq"), None), P("pipe", ("dp", "seq"), None)),
        check_vma=False,
    )
```
